512 devices in a mesh: grp: 8 (over x, core), dev: 64 (over z, y).
Axes of the slice: x: 4, y: 8, z: 8, core: 2. Of those that a mesh axis runs over, the one named last changes fastest.
Arguments:
- passages: bfloat16 [98304, 4096], P('dev'), may hold values from -6 to 6
- ckpt_weight: bfloat16 [4096, 4096], P('dev', 'grp'), may hold values from -0.09375 to 0.09375
- old_bank: bfloat16 [8192, 4096], P('dev', 'grp'), may hold values from -6 to 6
- touched: int32 [384], replicated, may hold values from 0 to 8191, as said below
- neg_owner: int32 [2048, 8], P('dev'), may hold values from 0 to 63, all different within a row; in each aligned block of 32 rows (0 to 31, 32 to 63, ...) at most 8 rows name the same one
- neg_row: int32 [2048, 8], P('dev'), may hold values from 0 to 127
- queries: bfloat16 [2048, 4096], P('dev', 'grp'), may hold values from -32 to 32
- positives: bfloat16 [2048, 4096], P('dev', 'grp'), may hold values from -64 to 64
Outputs:
- new_bank: bfloat16 [8192, 4096], P('dev', 'grp')
- losses: float32 [2048], P('dev')
- direction: float32 [2048, 4096], P('dev', 'grp')
The draws below stay inside these ranges and needn't reach their ends.
Inputs may be any that keep to these rules, and one draw needn't show every extreme that they name: `touched`: distinct bank rows. `neg_owner`: the queries of one index of dev name one bank shard at most 8 times, a bound that some block reaches; a query names 8 different shards.
All inputs are finite; a program needn't handle non-finite values.
Results may differ from the reference program's by a relative error of at most 0.00046.
Values may be sent and summed in bfloat16 or wider, within the bound.
A program may use at most 64 MiB of HBM per device.

```python
import math
import jax
import jax.numpy as jnp
import numpy as np
from jax import lax

D = 4096
PLEN = 256
NEG = 8
BANK_DEV = 128
Q_DEV = 32
OWNERS = 64
CAP = 8
PASSAGES = 384
TOKENS = 98304
BANK = 8192
QUERIES = 2048


def shared_rows(key):
    return jax.random.normal(key, (QUERIES, D), jnp.float32)


def draw_touched(key, part):
    key = jax.random.fold_in(key, 3)
    return jax.random.permutation(key, BANK)[:PASSAGES].astype(jnp.int32)


def draw_positives(key, part):
    base = shared_rows(key)
    return jnp.clip(base, -6.0, 6.0).astype(jnp.bfloat16)


def draw_queries(key, part):
    key = jax.random.fold_in(key, 7)
    noise = jnp.clip(jax.random.normal(key, (QUERIES, D), jnp.float32), -6.0, 6.0)
    return noise.astype(jnp.bfloat16)


def plant(array, own_key, smallest, top_value):
    extent = array.shape
    place = [jax.random.randint(jax.random.fold_in(own_key, axis), (), 0, extent[axis]) for axis in range(len(extent))]
    array = array.at[tuple(place)].set(smallest)
    longest = extent.index(max(extent))
    place[longest] = (place[longest] + 1) % extent[longest]
    return array.at[tuple(place)].set(top_value)


def level_of(stream_key, shape, pieces, least, largest):
    gain = 1.0
    for dim, blocks in pieces:
        heights = jax.random.uniform(jax.random.fold_in(jax.random.fold_in(stream_key, 6), dim), (blocks,), jnp.float32, least / len(pieces), largest / len(pieces))
        gain = gain * jnp.repeat(jnp.exp(heights), shape[dim] // blocks).reshape((-1,) + (1,) * (len(shape) - 1 - dim))
    return gain


def shared_out(own_key, own, number, rows, amount, top, most, skew):
    ranking = jax.random.permutation(own_key, amount)
    crowded, usual = shares(amount, rows * top, most, skew, True), shares(amount, rows * top, most, skew, False)
    places = jnp.arange(amount)

    def named(tallies, rotation):
        used = int((tallies > 0).sum())
        fixed = max(1, used // 4)
        moved = fixed + (places - fixed + rotation * (used - fixed)) % max(1, amount - fixed)
        return jnp.zeros((amount,), jnp.int32).at[ranking[jnp.where(places < fixed, places, moved)]].set(jnp.asarray(tallies, jnp.int32))

    tallies = jnp.where(number % 4 == 0, named(crowded, number // 4), named(usual, number - number // 4 - 1))
    mixed = jax.random.permutation(jax.random.fold_in(own, 3), amount)
    donor, receiver = mixed[0:amount // 2 * 2:2], mixed[1:amount // 2 * 2:2]
    room = jnp.minimum(tallies[donor] - 1, most - tallies[receiver]) // 2
    room = jnp.where((donor == ranking[0]) | (receiver == ranking[0]) | (tallies[receiver] == 0), 0, jnp.maximum(room, 0))
    moved = jax.random.randint(jax.random.fold_in(own, 4), (amount // 2,), 0, 1 << 20) % (room + 1)
    tallies = tallies.at[donor].add(-moved).at[receiver].add(moved)
    members = jnp.searchsorted(jnp.cumsum(tallies), jnp.arange(rows * top), side="right").astype(jnp.int32)
    table = members.reshape(top, rows).T
    table = table[jax.random.permutation(jax.random.fold_in(own, 1), rows)]
    rotation = jax.random.randint(jax.random.fold_in(own, 2), (rows, 1), 0, top)
    return jnp.take_along_axis(table, (jnp.arange(top)[None, :] + rotation) % top, axis=1)


def shares(amount, total, limit, skew, full):
    loads = [(1 << 20) // math.isqrt(grade ** skew) + 1 for grade in range(1, amount + 1)]
    largest = limit if full else min(limit, max(-(-total // amount), total * loads[0] // sum(loads)))
    least = 1 if total - largest >= amount - 1 else 0
    holding, rest = [largest] + [least] * (amount - 1), total - largest - least * (amount - 1)
    while rest > 0:
        free = [i for i in range(1, amount) if holding[i] < largest] or [i for i in range(1, amount) if holding[i] < limit]
        mass, remaining = sum([loads[i] for i in free]), rest
        for i in free:
            addition = min(limit - holding[i], max(1, remaining * loads[i] // mass), rest)
            holding[i] = holding[i] + addition
            rest = rest - addition
    return np.array(holding)


def centred(stream_key, dims, width, limit, pieces=(), held_as=jnp.bfloat16):
    entries = width * jax.random.normal(stream_key, dims, jnp.float32)
    if pieces:
        entries = entries * level_of(stream_key, dims, pieces, -0.22, 0.18)
    return jnp.clip(entries, -limit, limit).astype(held_as)


def setup_inputs(seed: int = 0) -> dict:
    keys = jax.random.split(jax.random.key(seed), 9)
    passages = centred(keys[0], (TOKENS, D), 1.0, 6.0, ((0, 64),))
    ckpt_weight = centred(keys[1], (D, D), D ** -0.5, 0.09375, ((0, 64), (1, 8)))
    old_bank = centred(keys[2], (BANK, D), 1.0, 6.0, ((0, 64), (1, 8)))
    touched = draw_touched(jax.random.fold_in(keys[8], 71), 0)
    neg_owner_keys = jax.random.split(jax.random.fold_in(keys[4], 1), QUERIES // Q_DEV)
    neg_owner_turns = jax.random.permutation(jax.random.fold_in(keys[4], 3), QUERIES // Q_DEV)
    neg_owner = jax.vmap(lambda own, number: shared_out(jax.random.fold_in(keys[4], 2), own, number, Q_DEV, OWNERS, NEG, CAP, 2))(neg_owner_keys, neg_owner_turns).reshape((QUERIES, NEG))
    neg_row = plant(jax.random.randint(keys[5], (QUERIES, NEG), 0, BANK_DEV), jax.random.fold_in(keys[5], 1), 0, BANK_DEV - 1).astype(jnp.int32)
    queries = draw_queries(jax.random.fold_in(keys[8], 71), 0)
    positives = draw_positives(jax.random.fold_in(keys[8], 71), 0)
    return dict(passages=passages, ckpt_weight=ckpt_weight, old_bank=old_bank, touched=touched, neg_owner=neg_owner, neg_row=neg_row, queries=queries, positives=positives)


def encode_passage(passage, ckpt_weight):
    preact = jnp.dot(passage, ckpt_weight, preferred_element_type=jnp.float32)
    return (lax.optimization_barrier(jnp.sum(jnp.tanh(preact), axis=0)) / math.sqrt(PLEN)).astype(jnp.bfloat16)

def reference(passages, ckpt_weight, old_bank, touched, neg_owner, neg_row, queries, positives):
    stacked = passages.reshape(PASSAGES, PLEN, D)

    def encode_step(passage):
        return encode_passage(passage, ckpt_weight)
    fresh = lax.map(encode_step, stacked)
    new_bank = old_bank.at[touched].set(fresh)
    global_ids = (neg_owner * BANK_DEV + neg_row).astype(jnp.int32)
    negatives = new_bank[global_ids]
    key_rows = jnp.concatenate([positives[:, None, :], negatives], axis=1).astype(jnp.float32)
    query_values = queries.astype(jnp.float32)
    exact = lax.Precision.HIGHEST
    dot_sums = jnp.einsum('qd,qkd->qk', query_values, key_rows, precision=exact)
    square_sums = jnp.einsum('qkd,qkd->qk', key_rows, key_rows, precision=exact)
    inverse = lax.rsqrt(square_sums / D + 1e-06)
    scores = dot_sums * inverse / math.sqrt(D)
    highest = lax.optimization_barrier(jnp.max(scores, axis=1, keepdims=True))
    weights = jnp.exp(scores - highest)
    summed = lax.optimization_barrier(jnp.sum(weights, axis=1, keepdims=True))
    probs = weights / summed
    losses = highest[:, 0] + jnp.log(summed[:, 0]) - scores[:, 0]
    target = (jnp.arange(NEG + 1) == 0).astype(jnp.float32)
    coefficient = (probs - target[None, :]) * inverse
    direction = jnp.einsum('qk,qkd->qd', coefficient, key_rows, precision=exact)
    return (new_bank, losses, direction)
```

```python
import math

import jax
import jax.numpy as jnp
from jax import lax
from jax.experimental import pallas as pl
from jax.experimental.pallas import tpu as pltpu
from jax.sharding import PartitionSpec as P

MESH = pl.DeviceIdType.MESH
F32, BF16, I32 = jnp.float32, jnp.bfloat16, jnp.int32

D = 4096
PLEN = 256
SIDE = 8
GRP = 8
NEG = 8
CAP = 8
QD = 32
BANK = 128
COLS = 512
HALF = 256
DEPTH = 64
TOK = 1536
NPAS = TOK // PLEN
REQ = QD * NEG
SLOTS = SIDE * SIDE * CAP


def iota(shape, dim):
    return lax.broadcasted_iota(I32, shape, dim)


def wrap(v):
    return lax.rem(v + 2 * SIDE, SIDE)


def rel(j):
    return (1 - 2 * (j % 2)) * ((j + 1) // 2)


def dot(a, b):
    return jnp.dot(a, b, preferred_element_type=F32)


def ones(mask):
    return jnp.where(mask, 1.0, 0.0).astype(BF16)


def spread(x):
    left = x[:, :128].reshape(64, 8, 128)
    right = x[:, 128:].reshape(64, 8, 128)
    return jnp.concatenate([left, right], axis=1).astype(BF16)


def joined(x):
    x = x.astype(F32)
    left = x[:, :8].reshape(SLOTS, 128)
    right = x[:, 8:].reshape(SLOTS, 128)
    return jnp.concatenate([left, right], axis=1).astype(BF16)


def kernel(
    pas, w, bank, touched, owner, row, queries, positives,
    new_bank, losses, direction,
    pas_a, pas_b, w_a, w_b, acc,
    v_bank, v_touched, v_owner, v_row, v_q, v_pos, v_new, v_dir,
    t1, r1, r1t, r2, sb0, sb1, rb0, rb1, rr0, rr1, fr0, fr1,
    sel0, sel1, mat0, mat1, nb0, nb1, stats,
    s_in, s_pas, s_own, w1s, w1r, w2s, w2r, qs, qr, as_, ar, fs, frs, gs, gr, s_out,
):
    d = lax.axis_index("dev")
    g = lax.axis_index("grp")
    z, y = d // SIDE, lax.rem(d, SIDE)

    def at(dz, dy):
        return {"dev": wrap(z + dz) * SIDE + wrap(y + dy)}

    def along(axis, k):
        return at(k, 0) if axis == 0 else at(0, k)

    def remote(src, dst, send, recv, to):
        return pltpu.make_async_remote_copy(src, dst, send, recv, device_id=to, device_id_type=MESH)

    small = [
        (owner, v_owner), (row, v_row), (touched, v_touched), (bank, v_bank), (queries, v_q), (positives, v_pos)
    ]
    loads = [pltpu.make_async_copy(a, b, s_in.at[i]) for i, (a, b) in enumerate(small)]
    for c in loads:
        c.start()
    own_a = pltpu.make_async_copy(w.at[:, pl.ds(0, HALF)], w_a.at[y // 2, z, y % 2], s_own.at[0])
    own_b = pltpu.make_async_copy(w.at[:, pl.ds(HALF, HALF)], w_b.at[z, y], s_own.at[1])
    own_a.start()
    own_b.start()

    barrier = pltpu.get_barrier_semaphore()
    for k in range(1, SIDE):
        pl.semaphore_signal(barrier, inc=1, device_id=at(k, 0), device_id_type=MESH)
        pl.semaphore_signal(barrier, inc=1, device_id=at(0, k), device_id_type=MESH)
    for k in range(1, GRP):
        pl.semaphore_signal(barrier, inc=1, device_id={"grp": lax.rem(g + k, GRP)}, device_id_type=MESH)

    def load_b(k):
        zz = wrap(z + k)
        return pltpu.make_async_copy(pas.at[:, pl.ds(pl.multiple_of(zz * COLS, COLS), COLS)], pas_b.at[zz], s_pas.at[zz])

    for j in range(SIDE):
        load_b(rel(j)).start()
    flip = 2 * (y % 2) - 1
    pairs = [lax.rem(y // 2 + k + 8, 4) for k in (0, flip, -flip, 2)]
    for m in pairs:
        for zz in range(SIDE):
            pltpu.make_async_copy(
                pas.at[:, pl.ds(pl.multiple_of(zz * COLS + m * 128, 128), 128)],
                pas_a.at[m, :, pl.ds(zz * 128, 128)],
                s_pas.at[SIDE + m],
            ).start()

    pl.semaphore_wait(barrier, 2 * (SIDE - 1) + GRP - 1)

    def block(h, zz, yy):
        return w_a.at[yy // 2, zz, lax.rem(yy, 2)] if h == 0 else w_b.at[zz, yy]

    def mine(h):
        return w.at[:, pl.ds(h * HALF, HALF)]

    def name(h, j, k):
        return block(h, wrap(z + j), wrap(y + k)) if h == 0 else block(h, wrap(z + k), wrap(y + j))

    ORDER1 = (1, -1, 2, -2, 3, -3, 4)

    def first(h, src, came, delta):
        i = h * 7 + ORDER1.index(came + delta)
        b = name(h, -came, 0)
        return remote(b if src is None else src, b, w1s.at[i], w1r.at[i], along(h, delta))

    def second(h, way, s, j):
        i = (h * 2 + (1 - way) // 2) * 4 + s - 1
        b = name(h, rel(j), -way * (s - 1))
        src = mine(h) if s == 1 and isinstance(j, int) and j == 0 else b
        return remote(src, b, w2s.at[i], w2r.at[i, j], along(1 - h, way))

    firsts = []

    def go(c):
        c.start()
        firsts.append(c)

    for delta in (1, -1):
        for h in range(2):
            go(first(h, mine(h), 0, delta))
    for h in range(2):
        for way in (1, -1):
            second(h, way, 1, 0).start()
    for delta in (2, -2):
        for h in range(2):
            go(first(h, mine(h), 0, delta))

    def got_first(h, came):
        i = h * 7 + ORDER1.index(came)
        b = name(h, -came, 0)
        remote(b, b, w1s.at[i], w1r.at[i], along(h, 1)).wait_recv()

    place = {1: 1, -1: 2, 2: 3, -2: 4, 3: 5, -3: 6, 4: 7}

    for c in loads[:2]:
        c.wait()
    own_col = jnp.concatenate([v_owner[:, j : j + 1] for j in range(NEG)], axis=0)
    row_col = jnp.concatenate([v_row[:, j : j + 1] for j in range(NEG)], axis=0)
    own_zy = own_col
    own_yz = lax.rem(own_col, SIDE) * SIDE + own_col // SIDE
    named = ones(own_yz == iota((REQ, 128), 1))
    before = dot(ones(iota((REQ, REQ), 0) > iota((REQ, REQ), 1)), named)
    rank = jnp.sum(named.astype(F32) * before, axis=1, keepdims=True).astype(I32)
    entry = jnp.where(rank == iota((REQ, 128), 1), (row_col + 1).astype(F32), 0.0).astype(BF16)
    table = lax.dot_general(named, entry, (((0,), (0,)), ((), ())), preferred_element_type=F32)
    t1[...] = table[: SIDE * SIDE].reshape(SIDE, SIDE, 128)
    r1[pl.ds(y, 1)] = t1[pl.ds(y, 1)]

    def ask1(k):
        return remote(t1.at[wrap(y + k)], r1.at[y], qs.at[k - 1], qr.at[k - 1], at(0, k))

    def ask2(k):
        return remote(r1t.at[wrap(z + k)], r2.at[z], qs.at[6 + k], qr.at[6 + k], at(k, 0))

    for k in range(1, SIDE):
        ask1(k).start()

    for came in (1, -1):
        for h in range(2):
            got_first(h, came)
            for way in (1, -1):
                second(h, way, 1, place[came]).start()
    for came in (2, -2):
        for h in range(2):
            got_first(h, came)
            go(first(h, None, came, 1 if came > 0 else -1))
            if came > 0:
                go(first(h, None, came, 2))
            for way in (1, -1):
                second(h, way, 1, place[came]).start()

    for c in loads[2:4]:
        c.wait()
    p384, q512 = iota((NPAS * 64, SLOTS), 0), iota((NPAS * 64, SLOTS), 1)
    blk, i_ = q512 // 8, lax.rem(q512, 8)
    ids = v_touched[...]
    hilo = jnp.concatenate(
        [(ids // BANK + 1).astype(F32), lax.rem(ids, BANK).astype(F32), jnp.zeros((6, NPAS * 64), F32)], axis=0
    ).astype(BF16)

    def masks(h, own_pos, sel, mat, nb):
        dev_of = blk if h == 0 else lax.rem(blk, SIDE) * SIDE + blk // SIDE
        perm = ones((dev_of * NPAS + i_ == p384) & (i_ < NPAS))
        where = dot(hilo, perm)
        hi, lo = where[0:1].astype(I32), where[1:2].astype(I32)
        hit = (own_col + 1 == hi) & (row_col == lo)
        mat[...] = ones(hit)
        some = jnp.sum(jnp.where(hit, 1.0, 0.0), axis=1, keepdims=True)
        slot = own_pos * CAP + rank
        sel[...] = ones((slot == iota((REQ, SLOTS), 1)) & (some < 0.5))
        nb[...] = ones((hi == d + 1) & (lo == iota((BANK, SLOTS), 0)))

    masks(0, own_zy, sel0, mat0, nb0)

    for k in range(1, SIDE):
        ask1(k).wait_recv()
    zy = iota((64, 64), 0)
    swap = ones(lax.rem(zy, SIDE) * SIDE + zy // SIDE == iota((64, 64), 1))
    r1t[...] = dot(swap, r1[...].reshape(64, 128).astype(BF16)).reshape(SIDE, SIDE, 128)
    r2[pl.ds(z, 1)] = r1t[pl.ds(z, 1)]
    for k in range(1, SIDE):
        ask2(k).start()

    for came in (3, -3, 4):
        for h in range(2):
            got_first(h, came)
            for way in (1, -1):
                second(h, way, 1, place[came]).start()

    masks(1, own_yz, sel1, mat1, nb1)
    own_a.wait()
    own_b.wait()

    for k in range(1, SIDE):
        ask2(k).wait_recv()

    def answer(h, sb):
        p, r = iota((SLOTS, 64), 0) // 8, iota((SLOTS, 64), 1)
        asker = lax.rem(p, SIDE) * SIDE + p // SIDE if h == 0 else p
        lines = dot(ones(asker == r), r2[...].reshape(64, 128).astype(BF16))
        own = lax.rem(iota((SLOTS, 128), 0), 8) == iota((SLOTS, 128), 1)
        want = jnp.sum(jnp.where(own, lines, 0.0), axis=1, keepdims=True).astype(I32)
        pick = ones(want == iota((SLOTS, BANK), 1) + 1)
        out = dot(pick, v_bank[:, h * HALF : (h + 1) * HALF])
        sb[...] = spread(out).reshape(SIDE, SIDE, 16, 128)

    answer(0, sb0)
    answer(1, sb1)
    rb0[pl.ds(y, 1)] = sb0[pl.ds(y, 1)]
    rb1[pl.ds(z, 1)] = sb1[pl.ds(z, 1)]

    def rows1(h, k):
        i = h * 7 + k - 1
        if h == 0:
            return remote(sb0.at[wrap(y + k)], rb0.at[y], as_.at[i], ar.at[i], at(0, k))
        return remote(sb1.at[wrap(z + k)], rb1.at[z], as_.at[i], ar.at[i], at(k, 0))

    def rows2(h, k):
        i = 14 + h * 7 + k - 1
        if h == 0:
            return remote(rb0.at[:, wrap(z + k)], rr0.at[z], as_.at[i], ar.at[i], at(k, 0))
        return remote(rb1.at[:, wrap(y + k)], rr1.at[y], as_.at[i], ar.at[i], at(0, k))

    PIECE = TOK // 4

    def loaded_b(k):
        load_b(k).wait()

    def loaded_a(m):
        pltpu.make_async_copy(pas_a.at[m], pas_a.at[m], s_pas.at[SIDE + m]).wait()

    def unit_a(m, rows):
        return dot(pas_a[m, rows, :], w_a[m].reshape(1024, HALF))

    def unit_b(k, rows):
        zz = wrap(z + k)
        return dot(pas_b[zz, rows, :], w_b[zz].reshape(COLS, HALF))

    def arrived(s, j):
        for h in range(2):
            for way in (1, -1):
                second(h, way, s, j).wait_recv()

    def forwards(s, j, ways):
        for h in range(2):
            for way in ways:
                second(h, way, s, j).start()

    def received(s, j, ways):
        i0 = s - 1
        for h in range(2):
            for way in (1, -1):
                i = (h * 2 + (1 - way) // 2) * 4 + i0
                b = name(h, rel(j), -way * s)
                if s < 4 or way in ways:
                    remote(b, b, w2s.at[i], w2r.at[i, j], along(1 - h, way)).wait_recv()
                    if way in ways and s < 4:
                        second(h, way, s + 1, j).start()

    def ring_step(s, compute_a, compute_b):
        def turn(t, ways):
            rows = pl.ds(pl.multiple_of(t * PIECE, PIECE), PIECE)
            received(s, 2 * t, ways)
            if compute_a is not None:
                compute_a(rows)
            received(s, 2 * t + 1, ways)
            if compute_b is not None:
                compute_b(rows)

        def loop(lo, hi, ways):
            lax.fori_loop(lo, hi, lambda t, c: (turn(t, ways), c)[1], 0)

        if s < 3:
            loop(0, 4, (1, -1))
        else:
            loop(0, 2, (1,))
            loop(2, 4, (-1,))

    left, right = pl.ds(0, HALF), pl.ds(HALF, HALF)

    def first_b(rows):
        acc[rows, right] = unit_b(0, rows)

    def first_a(rows):
        acc[rows, left] = unit_a(pairs[0], rows)

    def more_a(k):
        def run(rows):
            acc[rows, left] += unit_a(pairs[k], rows)

        return run

    def more_b(s):
        def run(rows):
            acc[rows, right] += unit_b(s, rows) + unit_b(-s, rows)

        return run

    loaded_b(0)
    ring_step(1, None, first_b)
    loaded_b(1)
    loaded_b(-1)
    loaded_a(pairs[0])
    ring_step(2, first_a, more_b(1))
    loaded_b(2)
    loaded_b(-2)
    loaded_a(pairs[1])
    ring_step(3, more_a(1), more_b(2))
    for h in range(2):
        for k in range(1, SIDE):
            rows1(h, k).start()
    loaded_b(3)
    loaded_b(-3)
    loaded_a(pairs[2])
    ring_step(4, more_a(2), more_b(3))
    loaded_b(4)
    loaded_a(pairs[3])

    enc_a, enc_b = [], []
    for i in range(NPAS):
        rows = pl.ds(i * PLEN, PLEN)
        enc_a.append(jnp.sum(jnp.tanh(acc[rows, left] + unit_a(pairs[3], rows)), axis=0, keepdims=True))
        enc_b.append(jnp.sum(jnp.tanh(acc[rows, right] + unit_b(4, rows)), axis=0, keepdims=True))

    def tile(enc):
        e = jnp.concatenate(enc + [jnp.zeros((2, HALF), F32)], axis=0) / math.sqrt(PLEN)
        return jnp.concatenate([e[:, :128], e[:, 128:]], axis=0).astype(BF16).reshape(1, 1, 16, 128)

    fr0[pl.ds(z, 1), pl.ds(y, 1)] = tile(enc_a)
    fr1[pl.ds(y, 1), pl.ds(z, 1)] = tile(enc_b)

    def fresh1(h, k):
        i = h * 7 + k - 1
        if h == 0:
            return remote(fr0.at[z, y], fr0.at[z, y], fs.at[i], frs.at[i], at(0, k))
        return remote(fr1.at[y, z], fr1.at[y, z], fs.at[i], frs.at[i], at(k, 0))

    def fresh2(h, k):
        i = 14 + h * 7 + k - 1
        if h == 0:
            return remote(fr0.at[z], fr0.at[z], fs.at[i], frs.at[i], at(k, 0))
        return remote(fr1.at[y], fr1.at[y], fs.at[i], frs.at[i], at(0, k))

    def each(make, what):
        for k in range(1, SIDE):
            for h in range(2):
                getattr(make(h, k), what)()

    each(fresh1, "start")
    each(rows1, "wait_recv")
    each(rows2, "start")
    rr0[pl.ds(z, 1)] = rb0[:, pl.ds(z, 1)].reshape(1, SIDE, 16, 128)
    rr1[pl.ds(y, 1)] = rb1[:, pl.ds(y, 1)].reshape(1, SIDE, 16, 128)
    each(fresh1, "wait_recv")
    each(fresh2, "start")
    each(fresh2, "wait_recv")

    outs = []
    fresh = []
    for h, (fr, nb) in enumerate(((fr0, nb0), (fr1, nb1))):
        rows_h = joined(fr[...].reshape(64, 16, 128))
        fresh.append(rows_h)
        hit = nb[...]
        some = jnp.sum(hit.astype(F32), axis=1, keepdims=True)
        cols = slice(h * HALF, (h + 1) * HALF)
        placed = jnp.where(some > 0.5, dot(hit, rows_h), v_bank[:, cols].astype(F32))
        v_new[:, cols] = placed.astype(BF16)
    outs.append(pltpu.make_async_copy(v_new, new_bank, s_out.at[0]))
    outs[0].start()
    patched = [dot(m[...], f) for m, f in zip((mat0, mat1), fresh, strict=True)]
    loads[4].wait()
    loads[5].wait()

    each(rows2, "wait_recv")
    negs = [
        dot(s[...], joined(r[...].reshape(64, 16, 128))) + p
        for s, r, p in zip((sel0, sel1), (rr0, rr1), patched, strict=True)
    ]
    keys = [v_pos[...].astype(F32)]
    for j in range(NEG):
        keys.append(jnp.concatenate([n[j * QD : (j + 1) * QD] for n in negs], axis=1))
    q = v_q[...].astype(F32)
    lane = iota((QD, 128), 1)
    st = jnp.zeros((QD, 128), F32)
    for k, key in enumerate(keys):
        st = jnp.where(lane == k, jnp.sum(q * key, axis=1, keepdims=True), st)
        st = jnp.where(lane == 64 + k, jnp.sum(key * key, axis=1, keepdims=True), st)
    stats[pl.ds(g, 1)] = st.reshape(1, QD, 128)

    def share(k):
        return remote(stats.at[g], stats.at[g], gs.at[k - 1], gr.at[k - 1], {"grp": lax.rem(g + k, GRP)})

    for k in range(1, GRP):
        share(k).start()
    for k in range(1, GRP):
        share(k).wait_recv()
    total = stats[0]
    for k in range(1, GRP):
        total = total + stats[k]
    dots = total[:, :64]
    squares = total[:, 64:]
    valid = iota((QD, 64), 1) < NEG + 1
    inverse = lax.rsqrt(squares / D + 1e-06)
    scores = dots * inverse / math.sqrt(D)
    highest = jnp.max(jnp.where(valid, scores, -jnp.inf), axis=1, keepdims=True)
    weights = jnp.where(valid, jnp.exp(scores - highest), 0.0)
    summed = jnp.sum(weights, axis=1, keepdims=True)
    loss = highest + jnp.log(summed) - scores[:, 0:1]
    target = jnp.where(iota((QD, 64), 1) == 0, 1.0, 0.0)
    coefficient = (weights / summed - target) * inverse
    grad = coefficient[:, 0:1] * keys[0]
    for k in range(1, NEG + 1):
        grad = grad + coefficient[:, k : k + 1] * keys[k]
    v_dir[...] = grad
    outs.append(pltpu.make_async_copy(v_dir, direction, s_out.at[1]))
    outs[1].start()
    eye = iota((QD, QD), 0) == iota((QD, QD), 1)
    losses[...] = jnp.sum(jnp.where(eye, loss, 0.0), axis=0, keepdims=True)

    for c in firsts:
        c.wait_send()
    for h in range(2):
        for way in range(2):
            for s in range(1, 5):
                sent = w_b.at[0] if s < 4 else w_b.at[0, pl.ds(0, 4)]
                pltpu.make_async_copy(sent, sent, w2s.at[(h * 2 + way) * 4 + s - 1]).wait()
    for k in range(1, SIDE):
        ask1(k).wait_send()
        ask2(k).wait_send()
    for make in (rows1, rows2, fresh1, fresh2):
        each(make, "wait_send")
    for k in range(1, GRP):
        share(k).wait_send()
    for c in outs:
        c.wait()


def body(passages, ckpt_weight, old_bank, touched, neg_owner, neg_row, queries, positives):
    anywhere = pl.BlockSpec(memory_space=pl.ANY)
    vmem = pl.BlockSpec(memory_space=pltpu.VMEM)
    dma = pltpu.SemaphoreType.DMA
    V = pltpu.VMEM
    slots = V((SIDE, SIDE, 16, 128), BF16)
    new_bank, losses, direction = pl.pallas_call(
        kernel,
        out_shape=(
            jax.ShapeDtypeStruct((BANK, COLS), BF16),
            jax.ShapeDtypeStruct((1, QD), F32),
            jax.ShapeDtypeStruct((QD, COLS), F32),
        ),
        in_specs=[anywhere] * 8,
        out_specs=(anywhere, vmem, anywhere),
        scratch_shapes=[
            V((4, TOK, 1024), BF16),
            V((SIDE, TOK, COLS), BF16),
            V((4, SIDE, 2, DEPTH, HALF), BF16),
            V((SIDE, SIDE, DEPTH, HALF), BF16),
            V((TOK, COLS), F32),
            V((BANK, COLS), BF16),
            V((1, NPAS * 64), I32),
            V((QD, NEG), I32),
            V((QD, NEG), I32),
            V((QD, COLS), BF16),
            V((QD, COLS), BF16),
            V((BANK, COLS), BF16),
            V((QD, COLS), F32),
            *[V((SIDE, SIDE, 128), F32)] * 4,
            *[slots] * 8,
            *[V((REQ, SLOTS), BF16)] * 4,
            *[V((BANK, SLOTS), BF16)] * 2,
            V((GRP, QD, 128), F32),
            dma((6,)),
            dma((12,)),
            dma((2,)),
            dma((14,)),
            dma((14,)),
            dma((16,)),
            dma((16, 8)),
            dma((14,)),
            dma((14,)),
            dma((28,)),
            dma((28,)),
            dma((28,)),
            dma((28,)),
            dma((7,)),
            dma((7,)),
            dma((2,)),
        ],
        compiler_params=pltpu.CompilerParams(
            collective_id=0, has_side_effects=True, vmem_limit_bytes=60 * 1024 * 1024
        ),
    )(passages, ckpt_weight, old_bank, touched.reshape(1, -1), neg_owner, neg_row, queries, positives)
    return new_bank, losses.reshape(-1), direction


def solution(mesh):
    return jax.shard_map(
        body,
        mesh=mesh,
        in_specs=(
            P("dev", None),
            P("dev", "grp"),
            P("dev", "grp"),
            P(),
            P("dev", None),
            P("dev", None),
            P("dev", "grp"),
            P("dev", "grp"),
        ),
        out_specs=(P("dev", "grp"), P("dev"), P("dev", "grp")),
        check_vma=False,
    )
```

```python
import math

import jax
import jax.numpy as jnp
from jax import lax
from jax.experimental import pallas as pl
from jax.experimental.pallas import tpu as pltpu
from jax.sharding import PartitionSpec as P

MESH = pl.DeviceIdType.MESH
F32, BF16, I32 = jnp.float32, jnp.bfloat16, jnp.int32

D = 4096
PLEN = 256
SIDE = 8
GRP = 8
NEG = 8
CAP = 8
QD = 32
BANK = 128
COLS = 512
HALF = 256
DEPTH = 64
TOK = 1536
NPAS = TOK // PLEN
REQ = QD * NEG
SLOTS = SIDE * SIDE * CAP


def iota(shape, dim):
    return lax.broadcasted_iota(I32, shape, dim)


def wrap(v):
    return lax.rem(v + 2 * SIDE, SIDE)


def rel(j):
    return (1 - 2 * (j % 2)) * ((j + 1) // 2)


def dot(a, b):
    return jnp.dot(a, b, preferred_element_type=F32)


def ones(mask):
    return jnp.where(mask, 1.0, 0.0).astype(BF16)


def spread(x):
    left = x[:, :128].reshape(64, 8, 128)
    right = x[:, 128:].reshape(64, 8, 128)
    return jnp.concatenate([left, right], axis=1).astype(BF16)


def joined(x):
    x = x.astype(F32)
    left = x[:, :8].reshape(-1, 128)
    right = x[:, 8:].reshape(-1, 128)
    return jnp.concatenate([left, right], axis=1).astype(BF16)


def kernel(
    pas, w, bank, touched, owner, row, queries, positives,
    new_bank, losses, direction,
    pas_a, pas_b, w_a, w_b, acc,
    v_bank, v_touched, v_owner, v_row, v_q, v_pos, v_new, v_dir,
    t1, r1, r1t, r2, sb0, sb1, rb0, rb1, rr0, rr1, fr0, fr1, fl0, fl1,
    sel0, sel1, mat0, mat1, nb0, nb1, stats,
    s_in, s_pas, s_own, w1s, w1r, w2s, w2r, qs, qr, as_, ar, fs, frs, gs, gr, s_out,
):
    d = lax.axis_index("dev")
    g = lax.axis_index("grp")
    z, y = d // SIDE, lax.rem(d, SIDE)

    def at(dz, dy):
        return {"dev": wrap(z + dz) * SIDE + wrap(y + dy)}

    def along(axis, k):
        return at(k, 0) if axis == 0 else at(0, k)

    def remote(src, dst, send, recv, to):
        return pltpu.make_async_remote_copy(src, dst, send, recv, device_id=to, device_id_type=MESH)

    small = [
        (owner, v_owner), (row, v_row), (touched, v_touched), (bank, v_bank), (queries, v_q), (positives, v_pos)
    ]
    loads = [pltpu.make_async_copy(a, b, s_in.at[i]) for i, (a, b) in enumerate(small)]
    for c in loads:
        c.start()
    own_a = pltpu.make_async_copy(w.at[:, pl.ds(0, HALF)], w_a.at[y // 2, z, y % 2], s_own.at[0])
    own_b = pltpu.make_async_copy(w.at[:, pl.ds(HALF, HALF)], w_b.at[z, y], s_own.at[1])
    own_a.start()
    own_b.start()

    barrier = pltpu.get_barrier_semaphore()
    for k in range(1, SIDE):
        pl.semaphore_signal(barrier, inc=1, device_id=at(k, 0), device_id_type=MESH)
        pl.semaphore_signal(barrier, inc=1, device_id=at(0, k), device_id_type=MESH)
    for k in range(1, GRP):
        pl.semaphore_signal(barrier, inc=1, device_id={"grp": lax.rem(g + k, GRP)}, device_id_type=MESH)

    def load_b(k):
        zz = wrap(z + k)
        return pltpu.make_async_copy(pas.at[:, pl.ds(pl.multiple_of(zz * COLS, COLS), COLS)], pas_b.at[zz], s_pas.at[zz])

    for j in range(SIDE):
        load_b(rel(j)).start()
    flip = 2 * (y % 2) - 1
    pairs = [lax.rem(y // 2 + k + 8, 4) for k in (0, flip, -flip, 2)]
    for m in pairs:
        for zz in range(SIDE):
            pltpu.make_async_copy(
                pas.at[:, pl.ds(pl.multiple_of(zz * COLS + m * 128, 128), 128)],
                pas_a.at[m, :, pl.ds(zz * 128, 128)],
                s_pas.at[SIDE + m],
            ).start()

    acc[:, :HALF] = jnp.zeros((TOK, HALF), F32)

    for c in loads[:2]:
        c.wait()
    eye = iota((QD, QD), 0) == iota((QD, QD), 1)

    def column(v):
        lines = v[...].astype(F32)
        parts = [jnp.sum(jnp.where(eye, lines[j : j + 1], 0.0), axis=1, keepdims=True) for j in range(NEG)]
        return jnp.concatenate(parts, axis=0).astype(I32)

    own_col, row_col = column(v_owner), column(v_row)
    own_zy = own_col
    own_yz = lax.rem(own_col, SIDE) * SIDE + own_col // SIDE
    named = ones(own_yz == iota((REQ, 128), 1))
    before = dot(ones(iota((REQ, REQ), 0) > iota((REQ, REQ), 1)), named)
    rank = jnp.sum(named.astype(F32) * before, axis=1, keepdims=True).astype(I32)
    entry = jnp.where(rank == iota((REQ, 128), 1), (row_col + 1).astype(F32), 0.0).astype(BF16)
    table = lax.dot_general(named, entry, (((0,), (0,)), ((), ())), preferred_element_type=F32)
    t1[...] = table[: SIDE * SIDE].reshape(SIDE, SIDE, 128)
    pl.semaphore_wait(barrier, 2 * (SIDE - 1) + GRP - 1)

    def block(h, zz, yy):
        return w_a.at[yy // 2, zz, lax.rem(yy, 2)] if h == 0 else w_b.at[zz, yy]

    def mine(h):
        return w.at[:, pl.ds(h * HALF, HALF)]

    def name(h, j, k):
        return block(h, wrap(z + j), wrap(y + k)) if h == 0 else block(h, wrap(z + k), wrap(y + j))

    ORDER1 = (1, -1, 2, -2, 3, -3, 4)

    def first(h, src, came, delta):
        i = h * 7 + ORDER1.index(came + delta)
        b = name(h, -came, 0)
        return remote(b if src is None else src, b, w1s.at[i], w1r.at[i], along(h, delta))

    def second(h, way, s, j):
        i = (h * 2 + (1 - way) // 2) * 4 + s - 1
        b = name(h, rel(j), -way * (s - 1))
        src = mine(h) if s == 1 and isinstance(j, int) and j == 0 else b
        return remote(src, b, w2s.at[i], w2r.at[i, j], along(1 - h, way))

    firsts = []

    def go(c):
        c.start()
        firsts.append(c)

    for delta in (1, -1):
        for h in range(2):
            go(first(h, mine(h), 0, delta))
    for h in range(2):
        for way in (1, -1):
            second(h, way, 1, 0).start()
    for delta in (2, -2):
        for h in range(2):
            go(first(h, mine(h), 0, delta))

    def got_first(h, came):
        i = h * 7 + ORDER1.index(came)
        b = name(h, -came, 0)
        remote(b, b, w1s.at[i], w1r.at[i], along(h, 1)).wait_recv()

    place = {1: 1, -1: 2, 2: 3, -2: 4, 3: 5, -3: 6, 4: 7}

    r1[pl.ds(y, 1)] = t1[pl.ds(y, 1)]

    def ask1(k):
        return remote(t1.at[wrap(y + k)], r1.at[y], qs.at[k - 1], qr.at[k - 1], at(0, k))

    def ask2(k):
        return remote(r1t.at[wrap(z + k)], r2.at[z], qs.at[6 + k], qr.at[6 + k], at(k, 0))

    for k in range(1, SIDE):
        ask1(k).start()

    for came in (1, -1):
        for h in range(2):
            got_first(h, came)
            for way in (1, -1):
                second(h, way, 1, place[came]).start()
    for came in (2, -2):
        for h in range(2):
            got_first(h, came)
            go(first(h, None, came, 1 if came > 0 else -1))
            if came > 0:
                go(first(h, None, came, 2))
            for way in (1, -1):
                second(h, way, 1, place[came]).start()

    for came in (3, -3, 4):
        for h in range(2):
            got_first(h, came)
            for way in (1, -1):
                second(h, way, 1, place[came]).start()

    def ask_on():
        for k in range(1, SIDE):
            ask1(k).wait_recv()
        zy = iota((64, 64), 0)
        swap = ones(lax.rem(zy, SIDE) * SIDE + zy // SIDE == iota((64, 64), 1))
        r1t[...] = dot(swap, r1[...].reshape(64, 128).astype(BF16)).reshape(SIDE, SIDE, 128)
        r2[pl.ds(z, 1)] = r1t[pl.ds(z, 1)]
        for k in range(1, SIDE):
            ask2(k).start()

    def masks(h, own_pos, sel, mat, nb):
        ids = v_touched[...].reshape(1, NPAS * 64)
        hi, lo = ids // BANK, lax.rem(ids, BANK)
        if h == 1:
            halves = jnp.concatenate([hi.astype(F32), lo.astype(F32), jnp.zeros((6, NPAS * 64), F32)], axis=0).astype(BF16)
            spot = iota((1, NPAS * 64), 1)
            line, within = spot // (SIDE * NPAS), lax.rem(spot, SIDE * NPAS)
            source = (within // NPAS * SIDE + line) * NPAS + lax.rem(within, NPAS)
            moved = dot(halves, ones(source == iota((NPAS * 64, NPAS * 64), 0)))
            hi, lo = moved[0:1].astype(I32), moved[1:2].astype(I32)
        hit = (own_col == hi) & (row_col == lo)
        mat[...] = ones(hit)
        some = jnp.sum(jnp.where(hit, 1.0, 0.0), axis=1, keepdims=True)
        slot = own_pos * CAP + rank
        sel[...] = ones((slot == iota((REQ, SLOTS), 1)) & (some < 0.5))
        nb[...] = ones((hi == d) & (lo == iota((BANK, NPAS * 64), 0)))

    def answer(h, sb):
        p = iota((SLOTS, 1), 0) // 8
        asker = lax.rem(p, SIDE) * SIDE + p // SIDE if h == 0 else p
        lines = dot(ones(asker == iota((SLOTS, 64), 1)), r2[...].reshape(64, 128).astype(BF16))
        own = lax.rem(iota((SLOTS, 128), 0), 8) == iota((SLOTS, 128), 1)
        want = jnp.sum(jnp.where(own, lines, 0.0), axis=1, keepdims=True).astype(I32)
        pick = ones(want == iota((SLOTS, BANK), 1) + 1)
        out = dot(pick, v_bank[:, h * HALF : (h + 1) * HALF])
        sb[...] = spread(out).reshape(SIDE, SIDE, 16, 128)

    def answer_0():
        for k in range(1, SIDE):
            ask2(k).wait_recv()
        answer(0, sb0)
        rb0[pl.ds(y, 1)] = sb0[pl.ds(y, 1)]

    def answer_1():
        answer(1, sb1)
        rb1[pl.ds(z, 1)] = sb1[pl.ds(z, 1)]

    def rows1(h, k):
        i = h * 7 + k - 1
        if h == 0:
            return remote(sb0.at[wrap(y + k)], rb0.at[y], as_.at[i], ar.at[i], at(0, k))
        return remote(sb1.at[wrap(z + k)], rb1.at[z], as_.at[i], ar.at[i], at(k, 0))

    def rows2(h, k):
        i = 14 + h * 7 + k - 1
        if h == 0:
            return remote(rb0.at[:, wrap(z + k)], rr0.at[z], as_.at[i], ar.at[i], at(k, 0))
        return remote(rb1.at[:, wrap(y + k)], rr1.at[y], as_.at[i], ar.at[i], at(0, k))

    def loaded_b(k):
        load_b(k).wait()

    def loaded_a(m):
        pltpu.make_async_copy(pas_a.at[m], pas_a.at[m], s_pas.at[SIDE + m]).wait()

    def piece_a(m, t, rows=slice(None)):
        return dot(
            pas_a[m, rows, pl.ds(pl.multiple_of(t * 256, 256), 256)], w_a[m, pl.ds(2 * t, 2)].reshape(256, HALF)
        )

    def piece_b(k, t, rows=slice(None)):
        zz = wrap(z + k)
        return dot(
            pas_b[zz, rows, pl.ds(pl.multiple_of(t * 256, 256), 256)], w_b[zz, pl.ds(4 * t, 4)].reshape(256, HALF)
        )

    def received(s, j, ways):
        for h in range(2):
            for way in (1, -1):
                i = (h * 2 + (1 - way) // 2) * 4 + s - 1
                b = name(h, rel(j), -way * s)
                if s < 4 or way in ways:
                    remote(b, b, w2s.at[i], w2r.at[i, j], along(1 - h, way)).wait_recv()
                    if way in ways and s < 4:
                        second(h, way, s + 1, j).start()

    left, right = pl.ds(0, HALF), pl.ds(HALF, HALF)

    def ring_step(s, k):
        def turn_a(j, c):
            received(s, j, (1, -1) if s < 3 else (1,))
            acc[:, left] += piece_a(pairs[k], j)
            return c

        def turn_b(j, c):
            received(s, j, (1, -1) if s < 3 else (-1,))
            acc[:, right] += piece_b((s - 1) * (1 - 2 * ((j - 4) // 2)), lax.rem(j, 2))
            return c

        lax.fori_loop(0, 4, turn_a, 0)
        lax.fori_loop(4, 8, turn_b, 0)

    for c in loads[2:4]:
        c.wait()
    between = {
        0: ask_on,
        1: lambda: masks(0, own_zy, sel0, mat0, nb0),
        3: lambda: masks(1, own_yz, sel1, mat1, nb1),
        5: answer_0,
        7: answer_1,
    }
    for j in range(SIDE):
        received(1, j, (1, -1))
        if j in between:
            between[j]()
    own_a.wait()
    own_b.wait()
    loaded_b(0)
    acc[:, right] = piece_b(0, 0) + piece_b(0, 1)
    loaded_b(1)
    loaded_b(-1)
    loaded_a(pairs[0])
    ring_step(2, 0)
    loaded_b(2)
    loaded_b(-2)
    loaded_a(pairs[1])
    ring_step(3, 1)
    for h in range(2):
        for k in range(1, SIDE):
            rows1(h, k).start()
    loaded_b(3)
    loaded_b(-3)
    loaded_a(pairs[2])
    ring_step(4, 2)
    loaded_b(4)
    loaded_a(pairs[3])

    enc_a, enc_b = [], []
    for i in range(NPAS):
        rows = pl.ds(i * PLEN, PLEN)
        last_a = acc[rows, left] + dot(pas_a[pairs[3], rows, :], w_a[pairs[3]].reshape(1024, HALF))
        enc_a.append(jnp.sum(jnp.tanh(last_a), axis=0, keepdims=True))
        zz = wrap(z + 4)
        last_b = acc[rows, right] + dot(pas_b[zz, rows, :], w_b[zz].reshape(COLS, HALF))
        enc_b.append(jnp.sum(jnp.tanh(last_b), axis=0, keepdims=True))

    def tile(enc):
        e = jnp.concatenate(enc + [jnp.zeros((2, HALF), F32)], axis=0) / math.sqrt(PLEN)
        return jnp.concatenate([e[:, :128], e[:, 128:]], axis=0).astype(BF16).reshape(1, 16, 128)

    fr0[pl.ds(y, 1)] = tile(enc_a)
    fr1[pl.ds(z, 1)] = tile(enc_b)

    def fresh1(h, k):
        i = h * 7 + k - 1
        if h == 0:
            return remote(fr0.at[y], fr0.at[y], fs.at[i], frs.at[i], at(0, k))
        return remote(fr1.at[z], fr1.at[z], fs.at[i], frs.at[i], at(k, 0))

    def fresh2(h, k):
        i = 14 + h * 7 + k - 1
        if h == 0:
            return remote(fl0.at[z], fl0.at[z], fs.at[i], frs.at[i], at(k, 0))
        return remote(fl1.at[y], fl1.at[y], fs.at[i], frs.at[i], at(0, k))

    def each(make, what):
        for k in range(1, SIDE):
            for h in range(2):
                getattr(make(h, k), what)()

    each(fresh1, "start")
    each(rows1, "wait_recv")
    each(rows2, "start")
    each(fresh1, "wait_recv")
    kept = iota((SIDE * NPAS, 1), 0)
    keep = ones(kept // NPAS * 8 + lax.rem(kept, NPAS) == iota((SIDE * NPAS, 64), 1))
    fl0[pl.ds(z, 1)] = dot(keep, joined(fr0[...])).astype(BF16).reshape(1, SIDE * NPAS, HALF)
    fl1[pl.ds(y, 1)] = dot(keep, joined(fr1[...])).astype(BF16).reshape(1, SIDE * NPAS, HALF)
    each(fresh2, "start")
    rr0[pl.ds(z, 1)] = rb0[:, pl.ds(z, 1)].reshape(1, SIDE, 16, 128)
    rr1[pl.ds(y, 1)] = rb1[:, pl.ds(y, 1)].reshape(1, SIDE, 16, 128)
    loads[4].wait()
    loads[5].wait()
    each(rows2, "wait_recv")
    old = [dot(m[...], joined(r[...].reshape(64, 16, 128))) for m, r in ((sel0, rr0), (sel1, rr1))]
    each(fresh2, "wait_recv")
    fresh = [f[...].reshape(NPAS * 64, HALF) for f in (fl0, fl1)]
    negs = [o + dot(m[...], f) for o, m, f in zip(old, (mat0, mat1), fresh, strict=True)]
    keys = [v_pos[...].astype(F32)]
    for j in range(NEG):
        keys.append(jnp.concatenate([n[j * QD : (j + 1) * QD] for n in negs], axis=1))
    q = v_q[...].astype(F32)
    lane = iota((QD, 128), 1)
    st = jnp.zeros((QD, 128), F32)
    for k, key in enumerate(keys):
        st = jnp.where(lane == k, jnp.sum(q * key, axis=1, keepdims=True), st)
        st = jnp.where(lane == 16 + k, jnp.sum(key * key, axis=1, keepdims=True), st)
    packed = st[0:8]
    for a in range(1, 4):
        packed = packed + pltpu.roll(st[8 * a : 8 * a + 8], 32 * a, 1)
    stats[pl.ds(g, 1)] = packed.reshape(1, 8, 128)

    def share(k):
        return remote(stats.at[g], stats.at[g], gs.at[k - 1], gr.at[k - 1], {"grp": lax.rem(g + k, GRP)})

    for k in range(1, GRP):
        share(k).start()

    for h, nb in enumerate((nb0, nb1)):
        hit = nb[...]
        some = jnp.sum(hit.astype(F32), axis=1, keepdims=True)
        cols = slice(h * HALF, (h + 1) * HALF)
        v_new[:, cols] = jnp.where(some > 0.5, dot(hit, fresh[h]), v_bank[:, cols].astype(F32)).astype(BF16)
    outs = [pltpu.make_async_copy(v_new, new_bank, s_out.at[0])]
    outs[0].start()

    for k in range(1, GRP):
        share(k).wait_recv()
    total = stats[0]
    for k in range(1, GRP):
        total = total + stats[k]
    dots = jnp.concatenate([total] + [pltpu.roll(total, 128 - 32 * a, 1) for a in range(1, 4)], axis=0)
    squares = pltpu.roll(dots, 112, 1)
    valid = lane < NEG + 1
    inverse = lax.rsqrt(squares / D + 1e-06)
    scores = dots * inverse / math.sqrt(D)
    highest = jnp.max(jnp.where(valid, scores, -jnp.inf), axis=1, keepdims=True)
    weights = jnp.where(valid, jnp.exp(scores - highest), 0.0)
    summed = jnp.sum(weights, axis=1, keepdims=True)
    loss = highest + jnp.log(summed) - scores[:, 0:1]
    target = jnp.where(lane == 0, 1.0, 0.0)
    coefficient = (weights / summed - target) * inverse
    grad = coefficient[:, 0:1] * keys[0]
    for k in range(1, NEG + 1):
        grad = grad + coefficient[:, k : k + 1] * keys[k]
    v_dir[...] = grad
    outs.append(pltpu.make_async_copy(v_dir, direction, s_out.at[1]))
    outs[1].start()
    losses[...] = jnp.sum(jnp.where(eye, loss, 0.0), axis=0, keepdims=True)

    for c in firsts:
        c.wait_send()
    for h in range(2):
        for way in range(2):
            for s in range(1, 5):
                sent = w_b.at[0] if s < 4 else w_b.at[0, pl.ds(0, 4)]
                pltpu.make_async_copy(sent, sent, w2s.at[(h * 2 + way) * 4 + s - 1]).wait()
    for k in range(1, SIDE):
        ask1(k).wait_send()
        ask2(k).wait_send()
    for make in (rows1, rows2, fresh1, fresh2):
        each(make, "wait_send")
    for k in range(1, GRP):
        share(k).wait_send()
    for c in outs:
        c.wait()


def place(a, b, c, a_out, b_out, c_out):
    a_out[...] = a[...]
    b_out[...] = b[...]
    c_out[...] = c[...]


def body(passages, ckpt_weight, old_bank, touched, neg_owner, neg_row, queries, positives):
    anywhere = pl.BlockSpec(memory_space=pl.ANY)
    vmem = pl.BlockSpec(memory_space=pltpu.VMEM)
    dma = pltpu.SemaphoreType.DMA
    V = pltpu.VMEM
    slots = V((SIDE, SIDE, 16, 128), BF16)
    new_bank, losses, direction = pl.pallas_call(
        kernel,
        out_shape=(
            jax.ShapeDtypeStruct((BANK, COLS), BF16),
            jax.ShapeDtypeStruct((1, QD), F32),
            jax.ShapeDtypeStruct((QD, COLS), F32),
        ),
        in_specs=[anywhere] * 8,
        out_specs=(anywhere, vmem, anywhere),
        scratch_shapes=[
            V((4, TOK, 1024), BF16),
            V((SIDE, TOK, COLS), BF16),
            V((4, SIDE, 2, DEPTH, HALF), BF16),
            V((SIDE, SIDE, DEPTH, HALF), BF16),
            V((TOK, COLS), F32),
            V((BANK, COLS), BF16),
            V((NPAS * 64,), I32),
            V((NEG, QD), I32),
            V((NEG, QD), I32),
            V((QD, COLS), BF16),
            V((QD, COLS), BF16),
            V((BANK, COLS), BF16),
            V((QD, COLS), F32),
            *[V((SIDE, SIDE, 128), F32)] * 4,
            *[slots] * 6,
            *[V((SIDE, 16, 128), BF16)] * 2,
            *[V((SIDE, SIDE * NPAS, HALF), BF16)] * 2,
            *[V((REQ, SLOTS), BF16)] * 2,
            *[V((REQ, NPAS * 64), BF16)] * 2,
            *[V((BANK, NPAS * 64), BF16)] * 2,
            V((GRP, 8, 128), F32),
            dma((6,)),
            dma((12,)),
            dma((2,)),
            dma((14,)),
            dma((14,)),
            dma((16,)),
            dma((16, 8)),
            dma((14,)),
            dma((14,)),
            dma((28,)),
            dma((28,)),
            dma((28,)),
            dma((28,)),
            dma((7,)),
            dma((7,)),
            dma((2,)),
        ],
        compiler_params=pltpu.CompilerParams(
            collective_id=0, has_side_effects=True, vmem_limit_bytes=60 * 1024 * 1024
        ),
    )(passages, ckpt_weight, old_bank, touched, neg_owner.T, neg_row.T, queries, positives)
    results = (new_bank, losses, direction)
    new_bank, losses, direction = pl.pallas_call(
        place,
        out_shape=tuple(jax.ShapeDtypeStruct(r.shape, r.dtype) for r in results),
        in_specs=[vmem] * 3,
        out_specs=(vmem,) * 3,
    )(*results)
    return new_bank, losses.reshape(-1), direction


def solution(mesh):
    return jax.shard_map(
        body,
        mesh=mesh,
        in_specs=(
            P("dev", None),
            P("dev", "grp"),
            P("dev", "grp"),
            P(),
            P("dev", None),
            P("dev", None),
            P("dev", "grp"),
            P("dev", "grp"),
        ),
        out_specs=(P("dev", "grp"), P("dev"), P("dev", "grp")),
        check_vma=False,
    )
```

```python
import math

import jax
import jax.numpy as jnp
from jax import lax
from jax.experimental import pallas as pl
from jax.experimental.pallas import tpu as pltpu
from jax.sharding import PartitionSpec as P

MESH = pl.DeviceIdType.MESH
F32, BF16, I32 = jnp.float32, jnp.bfloat16, jnp.int32

D = 4096
PLEN = 256
SIDE = 8
GRP = 8
NEG = 8
CAP = 8
QD = 32
BANK = 128
COLS = 512
HALF = 256
DEPTH = 64
TOK = 1536
NPAS = TOK // PLEN
REQ = QD * NEG
SLOTS = SIDE * SIDE * CAP


def iota(shape, dim):
    return lax.broadcasted_iota(I32, shape, dim)


def wrap(v):
    return lax.rem(v + 2 * SIDE, SIDE)


def rel(j):
    return (1 - 2 * (j % 2)) * ((j + 1) // 2)


def dot(a, b):
    return jnp.dot(a, b, preferred_element_type=F32)


def ones(mask):
    return jnp.where(mask, 1.0, 0.0).astype(BF16)


def spread(x):
    left = x[:, :128].reshape(-1, 8, 128)
    right = x[:, 128:].reshape(-1, 8, 128)
    return jnp.concatenate([left, right], axis=1).astype(BF16)


def joined(x):
    x = x.astype(F32)
    left = x[:, :8].reshape(-1, 128)
    right = x[:, 8:].reshape(-1, 128)
    return jnp.concatenate([left, right], axis=1).astype(BF16)


def kernel(
    pas, w, bank, touched, owner, row, queries, positives,
    new_bank, losses, direction,
    pas_a, pas_b, w_a, w_b, acc,
    v_bank, v_touched, v_owner, v_row, v_q, v_pos, v_new, v_dir,
    t0, t1, q0, q1, g0, g1, sb0, sb1, rr0, rr1, fr0, fr1, fl0, fl1,
    sel0, sel1, mat0, mat1, nb0, nb1, stats,
    s_in, s_pas, s_own, w1s, w1r, w2s, w2r, bs, br, qs, qr, as_, ar, fs, frs, gs, gr, s_out,
):
    d = lax.axis_index("dev")
    g = lax.axis_index("grp")
    z, y = d // SIDE, lax.rem(d, SIDE)

    def at(dz, dy):
        return {"dev": wrap(z + dz) * SIDE + wrap(y + dy)}

    def along(axis, k):
        return at(k, 0) if axis == 0 else at(0, k)

    def remote(src, dst, send, recv, to):
        return pltpu.make_async_remote_copy(src, dst, send, recv, device_id=to, device_id_type=MESH)

    small = [
        (owner, v_owner), (row, v_row), (touched, v_touched), (bank, v_bank), (queries, v_q), (positives, v_pos)
    ]
    loads = [pltpu.make_async_copy(a, b, s_in.at[i]) for i, (a, b) in enumerate(small)]
    for c in loads:
        c.start()
    own_a = pltpu.make_async_copy(w.at[:, pl.ds(0, HALF)], w_a.at[y // 2, z, y % 2], s_own.at[0])
    own_b = pltpu.make_async_copy(w.at[:, pl.ds(HALF, HALF)], w_b.at[z, y], s_own.at[1])
    own_a.start()
    own_b.start()
    own_g = [
        pltpu.make_async_copy(bank.at[:, pl.ds(0, HALF)], g0.at[y], s_own.at[2]),
        pltpu.make_async_copy(bank.at[:, pl.ds(HALF, HALF)], g1.at[z], s_own.at[3]),
    ]
    for c in own_g:
        c.start()

    barrier = pltpu.get_barrier_semaphore()
    for k in range(1, SIDE):
        pl.semaphore_signal(barrier, inc=1, device_id=at(k, 0), device_id_type=MESH)
        pl.semaphore_signal(barrier, inc=1, device_id=at(0, k), device_id_type=MESH)
    for k in range(1, GRP):
        pl.semaphore_signal(barrier, inc=1, device_id={"grp": lax.rem(g + k, GRP)}, device_id_type=MESH)

    def load_b(k):
        zz = wrap(z + k)
        return pltpu.make_async_copy(pas.at[:, pl.ds(pl.multiple_of(zz * COLS, COLS), COLS)], pas_b.at[zz], s_pas.at[zz])

    for j in range(SIDE):
        load_b(rel(j)).start()
    flip = 2 * (y % 2) - 1
    pairs = [lax.rem(y // 2 + k + 8, 4) for k in (0, flip, -flip, 2)]
    for m in pairs:
        for zz in range(SIDE):
            pltpu.make_async_copy(
                pas.at[:, pl.ds(pl.multiple_of(zz * COLS + m * 128, 128), 128)],
                pas_a.at[m, :, pl.ds(zz * 128, 128)],
                s_pas.at[SIDE + m],
            ).start()

    acc[:, :HALF] = jnp.zeros((TOK, HALF), F32)

    for c in loads[:2]:
        c.wait()
    eye = iota((QD, QD), 0) == iota((QD, QD), 1)

    def column(v):
        lines = v[...].astype(F32)
        parts = [jnp.sum(jnp.where(eye, lines[j : j + 1], 0.0), axis=1, keepdims=True) for j in range(NEG)]
        return jnp.concatenate(parts, axis=0).astype(I32)

    own_col, row_col = column(v_owner), column(v_row)
    own_zy = own_col
    own_yz = lax.rem(own_col, SIDE) * SIDE + own_col // SIDE
    named = ones(own_zy == iota((REQ, 128), 1))
    before = dot(ones(iota((REQ, REQ), 0) > iota((REQ, REQ), 1)), named)
    rank = jnp.sum(named.astype(F32) * before, axis=1, keepdims=True).astype(I32)
    entry = jnp.where(rank == iota((REQ, 128), 1), (row_col + 1).astype(F32), 0.0).astype(BF16)
    for t, one in ((t0, named), (t1, ones(own_yz == iota((REQ, 128), 1)))):
        table = lax.dot_general(one, entry, (((0,), (0,)), ((), ())), preferred_element_type=F32)
        t[...] = table[: SIDE * SIDE].reshape(SIDE, SIDE, 128)
    q0[pl.ds(z, 1)] = t0[pl.ds(z, 1)]
    q1[pl.ds(y, 1)] = t1[pl.ds(y, 1)]
    pl.semaphore_wait(barrier, 2 * (SIDE - 1) + GRP - 1)

    def block(h, zz, yy):
        return w_a.at[yy // 2, zz, lax.rem(yy, 2)] if h == 0 else w_b.at[zz, yy]

    def mine(h):
        return w.at[:, pl.ds(h * HALF, HALF)]

    def name(h, j, k):
        return block(h, wrap(z + j), wrap(y + k)) if h == 0 else block(h, wrap(z + k), wrap(y + j))

    ORDER1 = (1, -1, 2, -2, 3, -3, 4)

    def first(h, src, came, delta):
        i = h * 7 + ORDER1.index(came + delta)
        b = name(h, -came, 0)
        return remote(b if src is None else src, b, w1s.at[i], w1r.at[i], along(h, delta))

    def second(h, way, s, j):
        i = (h * 2 + (1 - way) // 2) * 4 + s - 1
        b = name(h, rel(j), -way * (s - 1))
        src = mine(h) if s == 1 and isinstance(j, int) and j == 0 else b
        return remote(src, b, w2s.at[i], w2r.at[i, j], along(1 - h, way))

    firsts = []

    def go(c):
        c.start()
        firsts.append(c)

    for delta in (1, -1):
        for h in range(2):
            go(first(h, mine(h), 0, delta))
    for h in range(2):
        for way in (1, -1):
            second(h, way, 1, 0).start()
    for delta in (2, -2):
        for h in range(2):
            go(first(h, mine(h), 0, delta))

    def got_first(h, came):
        i = h * 7 + ORDER1.index(came)
        b = name(h, -came, 0)
        remote(b, b, w1s.at[i], w1r.at[i], along(h, 1)).wait_recv()

    place = {1: 1, -1: 2, 2: 3, -2: 4, 3: 5, -3: 6, 4: 7}

    def ask(h, k):
        i = h * 7 + k - 1
        if h == 0:
            return remote(t0.at[wrap(z + k)], q0.at[z], qs.at[i], qr.at[i], at(k, 0))
        return remote(t1.at[wrap(y + k)], q1.at[y], qs.at[i], qr.at[i], at(0, k))

    def each(make, what):
        for k in range(1, SIDE):
            for h in range(2):
                getattr(make(h, k), what)()

    def shard(h, k, s, way):
        b = g0.at[wrap(y + k)] if h == 0 else g1.at[wrap(z + k)]
        return b if s < 4 else b.at[pl.ds(0 if way == 1 else 64, 64)]

    def pass_bank(h, way, s):
        i = (h * 2 + (1 - way) // 2) * 4 + s - 1
        b = shard(h, -way * (s - 1), s, way)
        src = bank.at[:, pl.ds(h * HALF, HALF)] if s == 1 else b
        return remote(src, b, bs.at[i], br.at[i], along(1 - h, way))

    def got_bank(s):
        for h in range(2):
            for way in (1, -1):
                i = (h * 2 + (1 - way) // 2) * 4 + s - 1
                b = shard(h, -way * s, s, way)
                remote(b, b, bs.at[i], br.at[i], along(1 - h, way)).wait_recv()

    def send_bank(s):
        for h in range(2):
            for way in (1, -1):
                pass_bank(h, way, s).start()

    def bank_on(s):
        got_bank(s)
        send_bank(s + 1)

    send_bank(1)
    each(ask, "start")

    for came in (1, -1):
        for h in range(2):
            got_first(h, came)
            for way in (1, -1):
                second(h, way, 1, place[came]).start()
    for came in (2, -2):
        for h in range(2):
            got_first(h, came)
            go(first(h, None, came, 1 if came > 0 else -1))
            if came > 0:
                go(first(h, None, came, 2))
            for way in (1, -1):
                second(h, way, 1, place[came]).start()

    for came in (3, -3, 4):
        for h in range(2):
            got_first(h, came)
            for way in (1, -1):
                second(h, way, 1, place[came]).start()

    def masks(h, own_pos, sel, mat, nb):
        ids = v_touched[...].reshape(1, NPAS * 64)
        hi, lo = ids // BANK, lax.rem(ids, BANK)
        if h == 1:
            halves = jnp.concatenate([hi.astype(F32), lo.astype(F32), jnp.zeros((6, NPAS * 64), F32)], axis=0).astype(BF16)
            spot = iota((1, NPAS * 64), 1)
            line, within = spot // (SIDE * NPAS), lax.rem(spot, SIDE * NPAS)
            source = (within // NPAS * SIDE + line) * NPAS + lax.rem(within, NPAS)
            moved = dot(halves, ones(source == iota((NPAS * 64, NPAS * 64), 0)))
            hi, lo = moved[0:1].astype(I32), moved[1:2].astype(I32)
        hit = (own_col == hi) & (row_col == lo)
        mat[...] = ones(hit)
        some = jnp.sum(jnp.where(hit, 1.0, 0.0), axis=1, keepdims=True)
        slot = own_pos * CAP + rank
        sel[...] = ones((slot == iota((REQ, SLOTS), 1)) & (some < 0.5))
        nb[...] = ones((hi == d) & (lo == iota((BANK, NPAS * 64), 0)))

    def answer(h, q, held, sb):
        p = iota((SLOTS, 1), 0) // CAP
        asked = lax.rem(p, SIDE) * SIDE + p // SIDE
        lines = dot(ones(asked == iota((SLOTS, 64), 1)), q[...].reshape(64, 128).astype(BF16))
        own = lax.rem(iota((SLOTS, 128), 0), CAP) == iota((SLOTS, 128), 1)
        want = jnp.sum(jnp.where(own, lines, 0.0), axis=1, keepdims=True).astype(I32)
        pick = ones(want == iota((SLOTS, BANK), 1) + 1)
        for o in range(SIDE):
            sb[:, o] = spread(dot(pick[o * 64 : (o + 1) * 64], held[o]))

    def answers():
        got_bank(4)
        each(ask, "wait_recv")
        for c in own_g:
            c.wait()
        answer(0, q0, g0, sb0)
        answer(1, q1, g1, sb1)
        rr0[pl.ds(z, 1)] = sb0[pl.ds(z, 1)]
        rr1[pl.ds(y, 1)] = sb1[pl.ds(y, 1)]

    def replies(h, k):
        i = h * 7 + k - 1
        if h == 0:
            return remote(sb0.at[wrap(z + k)], rr0.at[z], as_.at[i], ar.at[i], at(k, 0))
        return remote(sb1.at[wrap(y + k)], rr1.at[y], as_.at[i], ar.at[i], at(0, k))

    def loaded_b(k):
        load_b(k).wait()

    def loaded_a(m):
        pltpu.make_async_copy(pas_a.at[m], pas_a.at[m], s_pas.at[SIDE + m]).wait()

    def piece_a(m, t, rows=slice(None)):
        return dot(
            pas_a[m, rows, pl.ds(pl.multiple_of(t * 256, 256), 256)], w_a[m, pl.ds(2 * t, 2)].reshape(256, HALF)
        )

    def piece_b(k, t, rows=slice(None)):
        zz = wrap(z + k)
        return dot(
            pas_b[zz, rows, pl.ds(pl.multiple_of(t * 256, 256), 256)], w_b[zz, pl.ds(4 * t, 4)].reshape(256, HALF)
        )

    def received(s, j, ways):
        for h in range(2):
            for way in (1, -1):
                i = (h * 2 + (1 - way) // 2) * 4 + s - 1
                b = name(h, rel(j), -way * s)
                if s < 4 or way in ways:
                    remote(b, b, w2s.at[i], w2r.at[i, j], along(1 - h, way)).wait_recv()
                    if way in ways and s < 4:
                        second(h, way, s + 1, j).start()

    left, right = pl.ds(0, HALF), pl.ds(HALF, HALF)

    def ring_step(s, k):
        def turn_a(j, c):
            received(s, j, (1, -1) if s < 3 else (1,))
            acc[:, left] += piece_a(pairs[k], j)
            return c

        def turn_b(j, c):
            received(s, j, (1, -1) if s < 3 else (-1,))
            acc[:, right] += piece_b((s - 1) * (1 - 2 * ((j - 4) // 2)), lax.rem(j, 2))
            return c

        lax.fori_loop(0, 4, turn_a, 0)
        lax.fori_loop(4, 8, turn_b, 0)

    for c in loads[2:4]:
        c.wait()
    between = {
        2: lambda: masks(0, own_zy, sel0, mat0, nb0),
        7: lambda: bank_on(1),
        5: lambda: masks(1, own_yz, sel1, mat1, nb1),
    }
    for j in range(SIDE):
        received(1, j, (1, -1))
        if j in between:
            between[j]()
    own_a.wait()
    own_b.wait()
    loaded_b(0)
    acc[:, right] = piece_b(0, 0) + piece_b(0, 1)
    loaded_b(1)
    loaded_b(-1)
    loaded_a(pairs[0])
    ring_step(2, 0)
    bank_on(2)
    loaded_b(2)
    loaded_b(-2)
    loaded_a(pairs[1])
    ring_step(3, 1)
    bank_on(3)
    loaded_b(3)
    loaded_b(-3)
    loaded_a(pairs[2])
    ring_step(4, 2)
    loaded_b(4)
    loaded_a(pairs[3])

    enc_a, enc_b = [], []
    for i in range(NPAS):
        rows = pl.ds(i * PLEN, PLEN)
        last_a = acc[rows, left] + dot(pas_a[pairs[3], rows, :], w_a[pairs[3]].reshape(1024, HALF))
        enc_a.append(jnp.sum(jnp.tanh(last_a), axis=0, keepdims=True))
        zz = wrap(z + 4)
        last_b = acc[rows, right] + dot(pas_b[zz, rows, :], w_b[zz].reshape(COLS, HALF))
        enc_b.append(jnp.sum(jnp.tanh(last_b), axis=0, keepdims=True))

    def tile(enc):
        e = jnp.concatenate(enc + [jnp.zeros((2, HALF), F32)], axis=0) / math.sqrt(PLEN)
        return jnp.concatenate([e[:, :128], e[:, 128:]], axis=0).astype(BF16).reshape(1, 16, 128)

    fr0[pl.ds(y, 1)] = tile(enc_a)
    fr1[pl.ds(z, 1)] = tile(enc_b)

    def fresh1(h, k):
        i = h * 7 + k - 1
        if h == 0:
            return remote(fr0.at[y], fr0.at[y], fs.at[i], frs.at[i], at(0, k))
        return remote(fr1.at[z], fr1.at[z], fs.at[i], frs.at[i], at(k, 0))

    def fresh2(h, k):
        i = 14 + h * 7 + k - 1
        if h == 0:
            return remote(fl0.at[z], fl0.at[z], fs.at[i], frs.at[i], at(k, 0))
        return remote(fl1.at[y], fl1.at[y], fs.at[i], frs.at[i], at(0, k))

    each(fresh1, "start")
    answers()
    each(replies, "start")
    each(fresh1, "wait_recv")
    kept = iota((SIDE * NPAS, 1), 0)
    keep = ones(kept // NPAS * 8 + lax.rem(kept, NPAS) == iota((SIDE * NPAS, 64), 1))
    fl0[pl.ds(z, 1)] = dot(keep, joined(fr0[...])).astype(BF16).reshape(1, SIDE * NPAS, HALF)
    fl1[pl.ds(y, 1)] = dot(keep, joined(fr1[...])).astype(BF16).reshape(1, SIDE * NPAS, HALF)
    each(fresh2, "start")
    loads[4].wait()
    loads[5].wait()
    each(replies, "wait_recv")
    old = [dot(m[...], joined(r[...].reshape(64, 16, 128))) for m, r in ((sel0, rr0), (sel1, rr1))]
    each(fresh2, "wait_recv")
    fresh = [f[...].reshape(NPAS * 64, HALF) for f in (fl0, fl1)]
    negs = [o + dot(m[...], f) for o, m, f in zip(old, (mat0, mat1), fresh, strict=True)]
    keys = [v_pos[...].astype(F32)]
    for j in range(NEG):
        keys.append(jnp.concatenate([n[j * QD : (j + 1) * QD] for n in negs], axis=1))
    q = v_q[...].astype(F32)
    lane = iota((QD, 128), 1)
    st = jnp.zeros((QD, 128), F32)
    for k, key in enumerate(keys):
        st = jnp.where(lane == k, jnp.sum(q * key, axis=1, keepdims=True), st)
        st = jnp.where(lane == 16 + k, jnp.sum(key * key, axis=1, keepdims=True), st)
    packed = st[0:8]
    for a in range(1, 4):
        packed = packed + pltpu.roll(st[8 * a : 8 * a + 8], 32 * a, 1)
    stats[pl.ds(g, 1)] = packed.reshape(1, 8, 128)

    def share(k):
        return remote(stats.at[g], stats.at[g], gs.at[k - 1], gr.at[k - 1], {"grp": lax.rem(g + k, GRP)})

    for k in range(1, GRP):
        share(k).start()

    for h, nb in enumerate((nb0, nb1)):
        hit = nb[...]
        some = jnp.sum(hit.astype(F32), axis=1, keepdims=True)
        cols = slice(h * HALF, (h + 1) * HALF)
        v_new[:, cols] = jnp.where(some > 0.5, dot(hit, fresh[h]), v_bank[:, cols].astype(F32)).astype(BF16)
    outs = [pltpu.make_async_copy(v_new, new_bank, s_out.at[0])]
    outs[0].start()

    for k in range(1, GRP):
        share(k).wait_recv()
    total = stats[0]
    for k in range(1, GRP):
        total = total + stats[k]
    dots = jnp.concatenate([total] + [pltpu.roll(total, 128 - 32 * a, 1) for a in range(1, 4)], axis=0)
    squares = pltpu.roll(dots, 112, 1)
    valid = lane < NEG + 1
    inverse = lax.rsqrt(squares / D + 1e-06)
    scores = dots * inverse / math.sqrt(D)
    highest = jnp.max(jnp.where(valid, scores, -jnp.inf), axis=1, keepdims=True)
    weights = jnp.where(valid, jnp.exp(scores - highest), 0.0)
    summed = jnp.sum(weights, axis=1, keepdims=True)
    loss = highest + jnp.log(summed) - scores[:, 0:1]
    target = jnp.where(lane == 0, 1.0, 0.0)
    coefficient = (weights / summed - target) * inverse
    grad = coefficient[:, 0:1] * keys[0]
    for k in range(1, NEG + 1):
        grad = grad + coefficient[:, k : k + 1] * keys[k]
    v_dir[...] = grad
    outs.append(pltpu.make_async_copy(v_dir, direction, s_out.at[1]))
    outs[1].start()
    losses[...] = jnp.sum(jnp.where(eye, loss, 0.0), axis=0, keepdims=True)

    for c in firsts:
        c.wait_send()
    for h in range(2):
        for way in range(2):
            for s in range(1, 5):
                sent = w_b.at[0] if s < 4 else w_b.at[0, pl.ds(0, 4)]
                pltpu.make_async_copy(sent, sent, w2s.at[(h * 2 + way) * 4 + s - 1]).wait()
    for h in range(2):
        for way in (1, -1):
            for s in range(1, 5):
                pass_bank(h, way, s).wait_send()
    for make in (ask, replies, fresh1, fresh2):
        each(make, "wait_send")
    for k in range(1, GRP):
        share(k).wait_send()
    for c in outs:
        c.wait()


def place(a, b, c, a_out, b_out, c_out):
    a_out[...] = a[...]
    b_out[...] = b[...]
    c_out[...] = c[...]


def body(passages, ckpt_weight, old_bank, touched, neg_owner, neg_row, queries, positives):
    anywhere = pl.BlockSpec(memory_space=pl.ANY)
    vmem = pl.BlockSpec(memory_space=pltpu.VMEM)
    dma = pltpu.SemaphoreType.DMA
    V = pltpu.VMEM
    slots = V((SIDE, SIDE, 16, 128), BF16)
    new_bank, losses, direction = pl.pallas_call(
        kernel,
        out_shape=(
            jax.ShapeDtypeStruct((BANK, COLS), BF16),
            jax.ShapeDtypeStruct((1, QD), F32),
            jax.ShapeDtypeStruct((QD, COLS), F32),
        ),
        in_specs=[anywhere] * 8,
        out_specs=(anywhere, vmem, anywhere),
        scratch_shapes=[
            V((4, TOK, 1024), BF16),
            V((SIDE, TOK, COLS), BF16),
            V((4, SIDE, 2, DEPTH, HALF), BF16),
            V((SIDE, SIDE, DEPTH, HALF), BF16),
            V((TOK, COLS), F32),
            V((BANK, COLS), BF16),
            V((NPAS * 64,), I32),
            V((NEG, QD), I32),
            V((NEG, QD), I32),
            V((QD, COLS), BF16),
            V((QD, COLS), BF16),
            V((BANK, COLS), BF16),
            V((QD, COLS), F32),
            *[V((SIDE, SIDE, 128), F32)] * 4,
            *[V((SIDE, BANK, HALF), BF16)] * 2,
            *[slots] * 4,
            *[V((SIDE, 16, 128), BF16)] * 2,
            *[V((SIDE, SIDE * NPAS, HALF), BF16)] * 2,
            *[V((REQ, SLOTS), BF16)] * 2,
            *[V((REQ, NPAS * 64), BF16)] * 2,
            *[V((BANK, NPAS * 64), BF16)] * 2,
            V((GRP, 8, 128), F32),
            dma((6,)),
            dma((12,)),
            dma((4,)),
            dma((14,)),
            dma((14,)),
            dma((16,)),
            dma((16, 8)),
            dma((16,)),
            dma((16,)),
            dma((14,)),
            dma((14,)),
            dma((14,)),
            dma((14,)),
            dma((28,)),
            dma((28,)),
            dma((7,)),
            dma((7,)),
            dma((2,)),
        ],
        compiler_params=pltpu.CompilerParams(
            collective_id=0, has_side_effects=True, vmem_limit_bytes=60 * 1024 * 1024
        ),
    )(passages, ckpt_weight, old_bank, touched, neg_owner.T, neg_row.T, queries, positives)
    results = (new_bank, losses, direction)
    new_bank, losses, direction = pl.pallas_call(
        place,
        out_shape=tuple(jax.ShapeDtypeStruct(r.shape, r.dtype) for r in results),
        in_specs=[vmem] * 3,
        out_specs=(vmem,) * 3,
    )(*results)
    return new_bank, losses.reshape(-1), direction


def solution(mesh):
    return jax.shard_map(
        body,
        mesh=mesh,
        in_specs=(
            P("dev", None),
            P("dev", "grp"),
            P("dev", "grp"),
            P(),
            P("dev", None),
            P("dev", None),
            P("dev", "grp"),
            P("dev", "grp"),
        ),
        out_specs=(P("dev", "grp"), P("dev"), P("dev", "grp")),
        check_vma=False,
    )
```
